256 devices in a mesh: blk: 64 (over x_hi, y, z), dsplit: 4 (over x_lo, core).
Axes of the slice: x: 4 (x_hi: 2, x_lo: 2; x = x_hi * 2 + x_lo), y: 4, z: 8, core: 2. Of those that a mesh axis runs over, the one named last changes fastest.
Arguments:
- amplitudes: bfloat16 [1280, 8, 800], P('blk', None, 'dsplit'), may hold values from -6 to 6
- integrals: bfloat16 [8, 800, 65536], P(None, 'dsplit', 'blk'), may hold values from -0.078125 to 0.078125
- residual_in: float32 [1280, 65536], P('dsplit', 'blk'), may hold values from -6 to 6
- pair_list: int32 [1280, 2], P('dsplit'), may hold values from 0 to 99, as said below
- ab_list: int32 [65536, 2], P('blk'), may hold values from 0 to 799, as said below
Outputs:
- residual_out: float32 [1280, 65536], P('dsplit', 'blk')
The draws below stay inside these ranges and needn't reach their ends.
Inputs may be any that keep to these rules, and one draw needn't show every extreme that they name: `pair_list`: each row is a pair (i, j) of occupied orbitals with i <= j. `ab_list`: each row is a pair (a, b) of virtual orbitals with a <= b.
All inputs are finite; a program needn't handle non-finite values.
Results may differ from the reference program's by a relative error of at most 0.0003.
Values may be sent and summed in bfloat16 or wider, within the bound.
No kernel may reach another device: no remote copies, remote signals or barrier semaphores. Data moves between devices by JAX's collectives and lax.ppermute only.
A program may use at most 128 MiB of HBM per device.

```python
import jax
import jax.numpy as jnp

NOCC = 100
NVIR = 800
CSLAB = 8
NPAIR = 1280
AB = 65536


def draw_ordered(key, count, top):
    first_key, second_key, third_key = jax.random.split(key, 3)
    lower = jax.random.randint(first_key, (count,), 0, top)
    offset = jax.random.randint(second_key, (count,), 0, top) % (top - lower)
    same = jax.random.randint(third_key, (count,), 0, 4) == 0
    offset = jnp.where(same, 0, offset)
    upper = lower + offset
    lower = lower.at[0].set(0)
    upper = upper.at[0].set(top - 1)
    return jnp.stack([lower, upper], axis=1).astype(jnp.int32)


def draw_pair_list(key, part):
    key = jax.random.fold_in(key, 1)
    return draw_ordered(key, NPAIR, NOCC)


def draw_ab_list(key, part):
    key = jax.random.fold_in(key, 2)
    return draw_ordered(key, AB, NVIR)


def shard_levels(own_key, dims, cuts, least, high):
    def one(position, blocks):
        heights = jax.random.uniform(jax.random.fold_in(jax.random.fold_in(own_key, 6), position), (blocks,), jnp.float32, least / len(cuts), high / len(cuts))
        return jnp.repeat(jnp.exp(heights), dims[position] // blocks).reshape((-1,) + (1,) * (len(dims) - position - 1))

    level = one(*cuts[0])
    for cut in cuts[1:]:
        level = level * one(*cut)
    return level


def bell_draw(stream_key, extent, width, most, shards=(), dtype=jnp.bfloat16):
    values = width * jax.random.normal(stream_key, extent, jnp.float32)
    if shards:
        values = values * shard_levels(stream_key, extent, shards, -0.22, 0.18)
    return jnp.clip(values, -most, most).astype(dtype)


def setup_inputs(seed: int = 0) -> dict:
    key_of = jax.random.split(jax.random.key(seed), 6)
    return {
        "amplitudes": bell_draw(key_of[0], (NPAIR, CSLAB, NVIR), 1.0, 6.0, ((0, 64), (2, 4))),
        "integrals": bell_draw(key_of[1], (CSLAB, NVIR, AB), (CSLAB * NVIR) ** -0.5, 0.078125, ((1, 4), (2, 64))),
        "residual_in": bell_draw(key_of[2], (NPAIR, AB), 1.0, 6.0, ((0, 4), (1, 64)), jnp.float32),
        "pair_list": draw_pair_list(jax.random.fold_in(key_of[5], 71), 0),
        "ab_list": draw_ab_list(jax.random.fold_in(key_of[5], 71), 0),
    }


def pair_scale(pairs):
    return jnp.where(pairs[:, 0] == pairs[:, 1], jnp.float32(0.5), jnp.float32(1.0))


def reference(amplitudes, integrals, residual_in, pair_list, ab_list):
    left = amplitudes.reshape(amplitudes.shape[0], -1)
    right = integrals.reshape(-1, integrals.shape[2])
    ladder = jnp.dot(left, right, preferred_element_type=jnp.float32)
    weight = pair_scale(pair_list)[:, None] * pair_scale(ab_list)[None, :]
    return residual_in + weight * ladder
```

```python
import functools

import jax
import jax.numpy as jnp
from jax import lax
from jax.experimental import pallas as pl
from jax.experimental.pallas import tpu as pltpu
from jax.sharding import Mesh
from jax.sharding import PartitionSpec as P

XH, Y, Z, XL = 2, 4, 8, 2
BLK = ("xh", "y", "z")
DS = ("xl", "core")
VMEM = pl.BlockSpec(memory_space=pltpu.VMEM)
SMEM = pl.BlockSpec(memory_space=pltpu.SMEM)
F32, BF16, F16 = jnp.float32, jnp.bfloat16, jnp.float16
LIMIT = 48 * 1024 * 1024


def params():
    return pltpu.CompilerParams(vmem_limit_bytes=LIMIT)


def to_core(hop):
    return [(2 * y + k, 2 * ((y + 2 * k + hop) % Y) + y // 2) for y in range(Y) for k in range(2)]


def turn(n, step):
    return [(i, (i + step) % n) for i in range(n)]


def pack_pairs(place_ref, *refs):
    blocks, out_ref, held = refs[:4], refs[4], refs[5]
    for j in range(4):
        held[lax.rem(j + 4 - place_ref[0], 4)] = blocks[j][...]
    out_ref[...] = jnp.concatenate([held[0], held[3], held[2], held[1]], axis=0)


def pack_ring(place_ref, *refs):
    blocks, out_ref, held = refs[:Z], refs[Z], refs[Z + 1]
    for dz in range(Z):
        held[lax.rem(place_ref[1] + dz, Z)] = blocks[dz][...]
    out_ref[...] = jnp.concatenate([held[i] for i in range(Z)], axis=0)


def part_kernel(count, *refs):
    blocks, own_ref, other_ref, out_ref, held = refs[:count], *refs[count:]

    @pl.when(pl.program_id(0) == 0)
    def _():
        for part in range(2):
            held[part] = jnp.concatenate([b[part * 40:part * 40 + 40, :] for b in blocks], axis=0)

    total = jnp.dot(held[0], own_ref[...], preferred_element_type=F32)
    total += jnp.dot(held[1], other_ref[...], preferred_element_type=F32)
    out_ref[...] = total


def partial_ladder(blocks, own, other, width=256):
    count = len(blocks)
    rows, depth, columns = count * 40, own.shape[0], own.shape[1]
    whole = pl.BlockSpec(blocks[0].shape, lambda n: (0, 0))
    weights = pl.BlockSpec((depth, width), lambda n: (0, n))
    return pl.pallas_call(
        functools.partial(part_kernel, count),
        out_shape=jax.ShapeDtypeStruct((rows, columns), F32),
        grid=(columns // width,),
        in_specs=[whole] * count + [weights] * 2,
        out_specs=pl.BlockSpec((rows, width), lambda n: (0, n)),
        scratch_shapes=[pltpu.VMEM((2, rows, depth), BF16)],
        compiler_params=params(),
        cost_estimate=pl.CostEstimate(flops=4 * rows * depth * columns, bytes_accessed=4 * depth * columns, transcendentals=0),
    )(*blocks, own, other)


def last_kernel(place_ref, s0, s1, s2, s3, own_ref, other_ref, in_ref, row_ref, col_ref, *refs):
    remote, out_ref = refs[:Z], refs[Z]
    held, total = refs[Z + 1], refs[Z + 2]
    y, z = place_ref[0], place_ref[1]
    for j, slot in enumerate((s0, s1, s2, s3)):

        @pl.when(pl.program_id(0) == 0)
        def _(j=j, slot=slot):
            held[lax.rem(j + 4 - y, 4)] = slot[...]

    for dz in range(Z):
        total[lax.rem(z + dz, Z)] = remote[dz][...]
    for a, (mine, mate) in enumerate(((0, 2), (3, 1))):
        ladder = jnp.dot(held[mine], own_ref[...], preferred_element_type=F32)
        ladder += jnp.dot(held[mate], other_ref[...], preferred_element_type=F32)
        ladder += jnp.concatenate([total[i, a * 20:a * 20 + 20] for i in range(Z)], axis=0)
        rows = pl.ds(a * 160, 160)
        out_ref[rows, :] = in_ref[rows, :] + (row_ref[rows, :] * col_ref[...]) * ladder


def finish(place, slots, own, other, residual, row, col, remote, width=256):
    depth, columns = own.shape
    slot = pl.BlockSpec(slots[0].shape, lambda n: (0, 0))
    weights = pl.BlockSpec((depth, width), lambda n: (0, n))
    wide = pl.BlockSpec((residual.shape[0], width), lambda n: (0, n))
    return pl.pallas_call(
        last_kernel,
        out_shape=jax.ShapeDtypeStruct(residual.shape, F32),
        grid=(columns // width,),
        in_specs=[SMEM] + [slot] * 4 + [weights] * 2 + [wide]
        + [pl.BlockSpec(row.shape, lambda n: (0, 0)), pl.BlockSpec((1, width), lambda n: (0, n))]
        + [pl.BlockSpec((40, width), lambda n: (0, n))] * Z,
        out_specs=wide,
        scratch_shapes=[pltpu.VMEM((4, 160, depth), BF16), pltpu.VMEM((Z, 40, width), F32)],
        compiler_params=params(),
        cost_estimate=pl.CostEstimate(flops=4 * 320 * depth * columns, bytes_accessed=4 * depth * columns, transcendentals=0),
    )(place, *slots, own, other, residual, row, col, *remote)


def pair_scale(pairs):
    return jnp.where(pairs[:, 0] == pairs[:, 1], F32(0.5), F32(1.0))


def per_device(amplitudes, integrals, residual_in, pair_list, ab_list):
    xh, y, z, xl = (lax.axis_index(n) for n in ("xh", "y", "z", "xl"))
    place = jnp.stack([y, z]).astype(jnp.int32)
    row = pair_scale(pair_list)[:, None]
    col = pair_scale(ab_list)[None, :]

    mine = amplitudes.reshape(amplitudes.shape[0], -1)
    own = integrals.reshape(-1, integrals.shape[2])
    mates = lax.ppermute(mine, "xh", turn(2, 1))
    other = lax.ppermute(own, "core", turn(2, 1))
    leaves = xh != xl
    gone = jnp.where(leaves, mine, mates)
    kept = jnp.where(leaves, mates, mine)

    slots = [lax.ppermute(gone, ("y", "core"), to_core(j)) for j in range(4)]
    around = [kept] + [lax.ppermute(kept, "z", turn(Z, -dz)) for dz in range(1, Z)]

    block = pl.pallas_call(
        pack_pairs,
        out_shape=jax.ShapeDtypeStruct((80, 1600), BF16),
        in_specs=[SMEM] + [VMEM] * 4,
        out_specs=VMEM,
        scratch_shapes=[pltpu.VMEM((4, 20, 1600), BF16)],
        compiler_params=params(),
    )(place, *slots)
    stack = pl.pallas_call(
        pack_ring,
        out_shape=jax.ShapeDtypeStruct((160, 1600), BF16),
        in_specs=[SMEM] + [VMEM] * Z,
        out_specs=VMEM,
        scratch_shapes=[pltpu.VMEM((Z, 20, 1600), BF16)],
        compiler_params=params(),
    )(place, *around)

    ring = {0: block}
    for step in range(1, Z // 2):
        ring[step] = lax.ppermute(ring[step - 1], "z", turn(Z, -1))
        ring[-step] = lax.ppermute(ring[1 - step], "z", turn(Z, 1))
    ring[Z // 2] = lax.ppermute(ring[Z // 2 - 1], "z", turn(Z, -1))
    full = [lax.ppermute(stack, ("y", "core"), to_core(j)) for j in (0, 2, 1, 3)]
    full = [full[0], full[2], full[1], full[3]]

    remote = [None] * Z
    for group in ((0, 1, -1), (2, -2), (3, -3, 4)):
        part = partial_ladder([ring[d] for d in group], own, other).astype(F16)
        back = lax.ppermute(part, "xl", turn(XL, 1)).astype(F32)
        for n, d in enumerate(group):
            remote[d % Z] = back[40 * n:40 * n + 40]
    return finish(place, full, own, other, residual_in, row, col, remote)


def solution(mesh):
    fine = Mesh(mesh.devices.reshape(XH, Y, Z, XL, 2), BLK + DS)
    placed = (P(BLK, None, DS), P(None, DS, BLK), P(DS, BLK), P(DS, None), P(BLK, None))
    return jax.shard_map(per_device, mesh=fine, in_specs=placed, out_specs=P(DS, BLK), check_vma=False)
```

```python
import jax
import jax.numpy as jnp
from jax import lax
from jax.experimental import pallas as pl
from jax.experimental.pallas import tpu as pltpu
from jax.sharding import Mesh
from jax.sharding import PartitionSpec as P

XH, Y, Z, XL = 2, 4, 8, 2
BLK = ("xh", "y", "z")
DS = ("xl", "core")
VMEM = pl.BlockSpec(memory_space=pltpu.VMEM)
SMEM = pl.BlockSpec(memory_space=pltpu.SMEM)
F32, BF16, F16 = jnp.float32, jnp.bfloat16, jnp.float16
MIB = 1024 * 1024


def turn(n, step):
    return [(i, (i + step) % n) for i in range(n)]


def ring(x):
    route = [(2 * z + c, 2 * ((z + 2 * c - 1) % Z) + c) for z in range(Z) for c in range(2)]
    return lax.ppermute(x, ("z", "core"), route)


def swap(x):
    route = [(2 * y + c, 2 * (3 - y if c else y ^ 1) + c) for y in range(Y) for c in range(2)]
    return lax.ppermute(x, ("y", "core"), route)


def cross(x, flip, hop):
    route = [(x * Y + y, (x ^ flip) * Y + (y ^ (2 * hop))) for x in range(XH) for y in range(Y)]
    return lax.ppermute(x, ("xh", "y"), route)


def mate(x):
    return lax.ppermute(x, "core", turn(2, 1))


def trade(x):
    return lax.ppermute(x, "xl", turn(XL, 1)).astype(F32)


def pack_kernel(place_ref, s0, s1, s2, s3, out_ref, held):
    for n, slot in enumerate((s0, s1, s2, s3)):
        kind = jnp.bitwise_xor(place_ref[2], n // 2)
        side = jnp.bitwise_xor(place_ref[3], n % 2)
        held[2 * side + kind] = slot[...]
    out_ref[...] = jnp.concatenate([held[n] for n in range(4)], axis=0)


def pack(place, *slots):
    rows, depth = slots[0].shape
    return pl.pallas_call(
        pack_kernel,
        out_shape=jax.ShapeDtypeStruct((4 * rows, depth), BF16),
        in_specs=[SMEM] + [VMEM] * 4,
        out_specs=VMEM,
        scratch_shapes=[pltpu.VMEM((4, rows, depth), BF16)],
        compiler_params=pltpu.CompilerParams(vmem_limit_bytes=4 * MIB),
    )(place, *slots)


def join_kernel(mine_ref, mate_ref, out_ref):
    other = mate_ref[...]
    out_ref[...] = jnp.concatenate([mine_ref[...], jnp.concatenate([other[40:], other[:40]], axis=0)], axis=1)


def join(mine, other):
    return pl.pallas_call(
        join_kernel,
        out_shape=jax.ShapeDtypeStruct((mine.shape[0], 2 * mine.shape[1]), BF16),
        in_specs=[VMEM] * 2,
        out_specs=VMEM,
        compiler_params=pltpu.CompilerParams(vmem_limit_bytes=4 * MIB),
    )(mine, other)


def collect(count, *parts):
    def kernel(*refs):
        pieces = [r[at:at + count, :] for r, (_, at) in zip(refs, parts)]
        refs[-1][...] = jnp.concatenate(pieces, axis=0)

    return pl.pallas_call(
        kernel,
        out_shape=jax.ShapeDtypeStruct((count * len(parts), parts[0][0].shape[1]), F32),
        in_specs=[VMEM] * len(parts),
        out_specs=VMEM,
        compiler_params=pltpu.CompilerParams(vmem_limit_bytes=4 * MIB),
    )(*[p for p, _ in parts])


def last_kernel(place_ref, in_ref, row_ref, col_ref, *refs):
    h0, s0, h1, s1, h2, s2, h3, s3, h4, s4, c1, c2, c3, b0, b2, b3, b4, out_ref, total, done, sems = refs
    here, there = place_ref[0] % 2, 1 - place_ref[0] % 2
    z, turned = place_ref[1], place_ref[4]

    def put(half, shift, kept, at, back, start):
        value = kept[at:at + 20, :] + back[start:start + 20, :]
        total[half, lax.rem(z + shift + Z, Z)] = value

    put(here, 0, h0, 0, b0, 0)
    put(there, 0, s0, 0, b0, 20)
    put(here, 4, h4, 0, b4, 0)
    put(there, 4, s4, 0, b4, 20)
    for step, h, s, c, back, start in ((1, h1, s1, c1, b0, 40), (2, h2, s2, c2, b2, 0), (3, h3, s3, c3, b3, 0)):
        put(here, turned * step, h, 0, back, start)
        put(there, turned * step, s, 0, back, start + 20)
        put(here, -turned * step, c, 0, back, start + 40)
        put(there, -turned * step, c, 40, back, start + 60)
    copies = []
    for n in range(4):
        a, first = n // 2, 4 * (n % 2)
        rows = pl.ds(n * 80, 80)
        ladder = jnp.concatenate([total[a, i] for i in range(first, first + 4)], axis=0)
        done[rows, :] = in_ref[rows, :] + (row_ref[rows, :] * col_ref[...]) * ladder
        copies.append(pltpu.make_async_copy(done.at[rows], out_ref.at[rows], sems.at[n]))
        copies[-1].start()
    for copy in copies:
        copy.wait()


def finish(place, residual, row, col, parts):
    return pl.pallas_call(
        last_kernel,
        out_shape=jax.ShapeDtypeStruct(residual.shape, F32),
        in_specs=[SMEM] + [VMEM] * (3 + len(parts)),
        out_specs=pl.BlockSpec(memory_space=pl.ANY),
        scratch_shapes=[
            pltpu.VMEM((2, Z, 20, residual.shape[1]), F32),
            pltpu.VMEM(residual.shape, F32),
            pltpu.SemaphoreType.DMA((4,)),
        ],
        compiler_params=pltpu.CompilerParams(vmem_limit_bytes=12 * MIB),
    )(place, residual, row, col, *parts)


def pair_scale(pairs):
    return jnp.where(pairs[:, 0] == pairs[:, 1], F32(0.5), F32(1.0))


def per_device(amplitudes, integrals, residual_in, pair_list, ab_list):
    xh, y, z, xl, core = (lax.axis_index(n) for n in ("xh", "y", "z", "xl", "core"))
    place = jnp.stack([y, z, xh != xl, (y // 2) ^ core, 1 - 2 * core]).astype(jnp.int32)
    row = pair_scale(pair_list)[:, None]
    col = pair_scale(ab_list)[None, :]
    tie = lax.optimization_barrier

    mine = amplitudes.reshape(amplitudes.shape[0], -1)
    own = integrals.reshape(-1, integrals.shape[2])
    slots = [cross(mine, n // 2, n % 2) for n in (3, 2, 1)] + [mine]
    slots = slots[::-1]
    other = mate(own)
    slots, other = tie((slots, other))
    weights = jnp.concatenate([own, other], axis=0)

    def dot(x):
        return jnp.dot(x, weights, preferred_element_type=F32)

    def low(*parts):
        return collect(20, *parts).astype(F16)

    def share(h, s):
        return mate(collect(40, (h, 40), (s, 40)))

    mine = pack(place, *slots)
    held0 = join(mine, mate(mine))
    held1, swap0 = ring(held0), swap(held0[:40])
    held1, weights = tie((held1, weights))
    held2, swap1 = ring(held1), swap(held1)
    h0, s0, h1 = dot(held0[:40]), dot(swap0), dot(held1)
    held2, h0, s0, h1 = tie((held2, h0, s0, h1))
    held3, swap2 = ring(held2), swap(held2)
    s1, h2 = dot(swap1), dot(held2)
    c1 = share(h1, s1)
    goes0 = low((h0, 20), (s0, 20), (h1, 20), (s1, 20), (c1, 20), (c1, 60))
    held3, goes0, h2 = tie((held3, goes0, h2))
    swap3, held4 = swap(held3), ring(held3[:40])
    b0 = trade(goes0)
    s2, h3 = dot(swap2), dot(held3)
    held4, s2, h3 = tie((held4, s2, h3))
    swap4 = swap(held4)
    c2 = share(h2, s2)
    b2 = trade(low((h2, 20), (s2, 20), (c2, 20), (c2, 60)))
    h4, s3 = dot(held4), dot(swap3)
    c3 = share(h3, s3)
    swap4, c2, c3, h4 = tie((swap4, c2, c3, h4))
    b3 = trade(low((h3, 20), (s3, 20), (c3, 20), (c3, 60)))
    s4 = dot(swap4)
    b4 = trade(low((h4, 20), (s4, 20)))
    parts = (h0, s0, h1, s1, h2, s2, h3, s3, h4, s4, c1, c2, c3, b0, b2, b3, b4)
    return finish(place, residual_in, row, col, parts)


def solution(mesh):
    fine = Mesh(mesh.devices.reshape(XH, Y, Z, XL, 2), BLK + DS)
    placed = (P(BLK, None, DS), P(None, DS, BLK), P(DS, BLK), P(DS, None), P(BLK, None))
    return jax.shard_map(per_device, mesh=fine, in_specs=placed, out_specs=P(DS, BLK), check_vma=False)
```

```python
import jax
import jax.numpy as jnp
from jax import lax
from jax.experimental import pallas as pl
from jax.experimental.pallas import tpu as pltpu
from jax.sharding import Mesh
from jax.sharding import PartitionSpec as P

XH, Y, Z, XL = 2, 4, 8, 2
BLK = ("xh", "y", "z")
DS = ("xl", "core")
VMEM = pl.BlockSpec(memory_space=pltpu.VMEM)
F32, BF16, F16 = jnp.float32, jnp.bfloat16, jnp.float16
MIB = 1024 * 1024


def limit(size):
    return pltpu.CompilerParams(vmem_limit_bytes=size * MIB)


def turn(n, step):
    return [(i, (i + step) % n) for i in range(n)]


def up(x):
    return lax.ppermute(x, "z", turn(Z, -1))


def down(x):
    return lax.ppermute(x, "z", turn(Z, 1))


def either(x):
    route = [(2 * z + c, 2 * ((z + 2 * c - 1) % Z) + c) for z in range(Z) for c in range(2)]
    return lax.ppermute(x, ("z", "core"), route)


def swap(x):
    route = [(2 * y + c, 2 * (3 - y if c else y ^ 1) + c) for y in range(Y) for c in range(2)]
    return lax.ppermute(x, ("y", "core"), route)


def spread(x, flip):
    def at(x, y, c):
        return (x * Y + y) * 2 + c

    route = [(at(x, y, k), at(x ^ flip, y % 2 + 2 * k, y // 2)) for x in range(XH) for y in range(Y) for k in range(2)]
    return lax.ppermute(x, ("xh", "y", "core"), route)


def mate(x):
    return lax.ppermute(x, "core", turn(2, 1))


def trade(x):
    return lax.ppermute(x, "xl", turn(XL, 1))


def choose(first, pairs, axis, out_ref):
    for order, pair in enumerate((pairs, pairs[::-1])):

        @pl.when(first == order)
        def _(pair=pair):
            out_ref[...] = jnp.concatenate([r[...] for r in pair], axis=axis)


def local_call(kernel, shapes, *operands):
    return pl.pallas_call(
        kernel,
        out_shape=[jax.ShapeDtypeStruct(s, BF16) for s in shapes],
        in_specs=[VMEM] * len(operands),
        out_specs=[VMEM] * len(shapes),
        compiler_params=limit(8),
    )(*operands)


def join_kernel(mine_ref, mate_ref, out_ref):
    away = lax.axis_index("y") // 2 != lax.axis_index("core")
    choose(away.astype(jnp.int32), (mine_ref, mate_ref), 1, out_ref)


def pack_kernel(far_ref, near_ref, out_ref):
    away = lax.axis_index("xh") != lax.axis_index("xl")
    choose(away.astype(jnp.int32), (near_ref, far_ref), 0, out_ref)


def pair_kernel(up_ref, down_ref, out_ref, pick_ref):
    out_ref[...] = jnp.concatenate([up_ref[...], down_ref[...]], axis=0)
    for order, ref in enumerate((up_ref, down_ref)):

        @pl.when(lax.axis_index("core") == order)
        def _(ref=ref):
            pick_ref[...] = ref[...]


def stack(*parts):
    def kernel(*refs):
        refs[-1][...] = jnp.concatenate([r[...] for r in refs[:-1]], axis=0)

    return pl.pallas_call(
        kernel,
        out_shape=jax.ShapeDtypeStruct((sum(p.shape[0] for p in parts), parts[0].shape[1]), BF16),
        in_specs=[VMEM] * len(parts),
        out_specs=VMEM,
        compiler_params=limit(8),
    )(*parts)


def halves(*parts):
    depth = parts[0].shape[1] // 2

    def kernel(*refs):
        whole = jnp.concatenate([r[...] for r in refs[:-2]], axis=0)
        refs[-2][...] = whole[:, :depth]
        refs[-1][...] = whole[:, depth:]

    return local_call(kernel, [(sum(p.shape[0] for p in parts), depth)] * 2, *parts)


def low(*parts):
    def kernel(*refs):
        refs[-1][...] = jnp.concatenate([r[at:at + 20, :] for r, (_, at) in zip(refs, parts)], axis=0)

    rows = pl.pallas_call(
        kernel,
        out_shape=jax.ShapeDtypeStruct((20 * len(parts), parts[0][0].shape[1]), F32),
        in_specs=[VMEM] * len(parts),
        out_specs=VMEM,
        compiler_params=limit(8),
    )(*[p for p, _ in parts])
    return rows.astype(F16)


def last_kernel(in_ref, row_ref, col_ref, *refs):
    m0, m1, m2, m3, m4, b0, b2, b3, b4, out_ref, total, done, sems = refs
    here, z = lax.axis_index("y") % 2, lax.axis_index("z")
    there = 1 - here

    def put(half, shift, kept, at, back, start):
        value = kept[at:at + 20, :] + back[start:start + 20, :]
        total[half, lax.rem(z + shift + Z, Z)] = value

    put(here, 0, m0, 0, b0, 0)
    put(there, 0, m0, 40, b0, 20)
    for step, h, at, b, start, s, back in ((1, m0, 80, b0, 40, m1, (b0, 80)), (2, m1, 80, b2, 0, m2, (b2, 40)), (3, m2, 80, b2, 80, m3, (b3, 0))):
        put(here, step, h, at, b, start)
        put(here, -step, h, at + 40, b, start + 20)
        put(there, step, s, 0, back[0], back[1])
        put(there, -step, s, 40, back[0], back[1] + 20)
    put(here, 4, m3, 80, b3, 40)
    put(there, 4, m4, 0, b4, 0)
    copies = []
    for n in range(4):
        a, first = n // 2, 4 * (n % 2)
        rows = pl.ds(n * 80, 80)
        ladder = jnp.concatenate([total[a, i] for i in range(first, first + 4)], axis=0)
        done[rows, :] = in_ref[rows, :] + (row_ref[rows, :1] * scale(col_ref[...])) * ladder
        copies.append(pltpu.make_async_copy(done.at[rows], out_ref.at[rows], sems.at[n]))
        copies[-1].start()
    for copy in copies:
        copy.wait()


def finish(residual, row, col, parts):
    return pl.pallas_call(
        last_kernel,
        out_shape=jax.ShapeDtypeStruct(residual.shape, F32),
        in_specs=[VMEM] * (3 + len(parts)),
        out_specs=pl.BlockSpec(memory_space=pl.ANY),
        scratch_shapes=[
            pltpu.VMEM((2, Z, 20, residual.shape[1]), F32),
            pltpu.VMEM(residual.shape, F32),
            pltpu.SemaphoreType.DMA((4,)),
        ],
        compiler_params=limit(12),
    )(residual, row, col, *parts)


def fetch(x):
    def kernel(x_ref, out_ref, sem):
        copy = pltpu.make_async_copy(x_ref, out_ref, sem)
        copy.start()
        copy.wait()

    return pl.pallas_call(
        kernel,
        out_shape=jax.ShapeDtypeStruct(x.shape, x.dtype),
        in_specs=[pl.BlockSpec(memory_space=pl.ANY)],
        out_specs=VMEM,
        scratch_shapes=[pltpu.SemaphoreType.DMA],
        compiler_params=limit(1),
    )(x)


def scale(pairs):
    return jnp.where(pairs[0:1, :] == pairs[1:2, :], F32(0.5), F32(1.0))


def row_scale(pairs):
    count = pairs.shape[1]

    def kernel(pairs_ref, out_ref):
        out_ref[...] = jnp.broadcast_to(scale(pairs_ref[...]), (128, count)).T

    return pl.pallas_call(
        kernel,
        out_shape=jax.ShapeDtypeStruct((count, 128), F32),
        in_specs=[VMEM],
        out_specs=VMEM,
        compiler_params=limit(4),
    )(pairs)


def per_device(amplitudes, integrals, residual_in, pair_list, ab_list):
    tie = lax.optimization_barrier

    mine = amplitudes.reshape(amplitudes.shape[0], -1)
    own = integrals.reshape(-1, integrals.shape[2])
    pairs, depth = mine.shape
    block, double = (2 * pairs, 2 * depth), (4 * pairs, 2 * depth)

    mates, own = tie((mate(mine), own))
    (both,) = local_call(join_kernel, [(pairs, 2 * depth)], mine, mates)
    slots = spread(both, 1), spread(both, 0)
    other = mate(own)
    (held,) = local_call(pack_kernel, [block], *slots)

    def dot(*parts):
        left, right = halves(*parts)
        total = jnp.dot(left, own, preferred_element_type=F32)
        return total + jnp.dot(right, second, preferred_element_type=F32)

    above, below = up(held), down(held)
    swap0 = swap(held)
    above, below, second = tie((above, below, fetch(other)))
    old = above, below
    above, below = up(above), down(below)
    beside = stack(*old)
    swap1 = swap(beside)
    m0 = dot(held, swap0, beside)
    above, below, m0 = tie((above, below, m0))
    old = above, below
    above, below = up(above), down(below)
    beside = stack(*old)
    swap2 = swap(beside)
    m1 = dot(swap1, beside)
    goes0 = low((m0, 20), (m0, 60), (m0, 100), (m0, 140), (m1, 20), (m1, 60))
    above, below, m1, goes0 = tie((above, below, m1, goes0))
    beside, pick = local_call(pair_kernel, [double, block], above, below)
    opposite = either(pick)
    swap3 = swap(beside)
    b0 = trade(goes0)
    m2 = dot(swap2, beside)
    goes2 = low((m1, 100), (m1, 140), (m2, 20), (m2, 60), (m2, 100), (m2, 140))
    opposite, m2, goes2 = tie((opposite, m2, goes2))
    swap4 = swap(opposite)
    b2 = trade(goes2)
    m3 = dot(swap3, opposite)
    goes3 = low((m3, 20), (m3, 60), (m3, 100))
    swap4, m3, goes3 = tie((swap4, m3, goes3))
    b3 = trade(goes3)
    m4 = dot(swap4)
    goes4, pair_list, ab_list = tie((low((m4, 20)), pair_list.T, ab_list.T))
    b4 = trade(goes4)
    row = row_scale(pair_list)
    back = [b.astype(F32) for b in (b0, b2, b3, b4)]
    return finish(residual_in, row, ab_list, (m0, m1, m2, m3, m4, *back))


def solution(mesh):
    fine = Mesh(mesh.devices.reshape(XH, Y, Z, XL, 2), BLK + DS)
    placed = (P(BLK, None, DS), P(None, DS, BLK), P(DS, BLK), P(DS, None), P(BLK, None))
    return jax.shard_map(per_device, mesh=fine, in_specs=placed, out_specs=P(DS, BLK), check_vma=False)
```

```python
import jax
import jax.numpy as jnp
from jax import lax
from jax.experimental import pallas as pl
from jax.experimental.pallas import tpu as pltpu
from jax.sharding import Mesh
from jax.sharding import PartitionSpec as P

XH, Y, Z, XL = 2, 4, 8, 2
BLK = ("xh", "y", "z")
DS = ("xl", "core")
VMEM = pl.BlockSpec(memory_space=pltpu.VMEM)
F32, BF16, F16 = jnp.float32, jnp.bfloat16, jnp.float16
MIB = 1024 * 1024


def limit(size):
    return pltpu.CompilerParams(vmem_limit_bytes=size * MIB)


def turn(n, step):
    return [(i, (i + step) % n) for i in range(n)]


def up(x):
    return lax.ppermute(x, "z", turn(Z, -1))


def down(x):
    return lax.ppermute(x, "z", turn(Z, 1))


def either(x):
    route = [(2 * z + c, 2 * ((z + 2 * c - 1) % Z) + c) for z in range(Z) for c in range(2)]
    return lax.ppermute(x, ("z", "core"), route)


def swap(x):
    route = [(2 * y + c, 2 * (3 - y if c else y ^ 1) + c) for y in range(Y) for c in range(2)]
    return lax.ppermute(x, ("y", "core"), route)


def spread(x, flip):
    def at(x, y, c):
        return (x * Y + y) * 2 + c

    route = [(at(x, y, k), at(x ^ flip, y % 2 + 2 * k, y // 2)) for x in range(XH) for y in range(Y) for k in range(2)]
    return lax.ppermute(x, ("xh", "y", "core"), route)


def mate(x):
    return lax.ppermute(x, "core", turn(2, 1))


def trade(x):
    return lax.ppermute(x, "xl", turn(XL, 1))


def choose(first, pairs, axis, out_ref):
    for order, pair in enumerate((pairs, pairs[::-1])):

        @pl.when(first == order)
        def _(pair=pair):
            out_ref[...] = jnp.concatenate(pair, axis=axis)


def local_call(kernel, shapes, *operands):
    return pl.pallas_call(
        kernel,
        out_shape=[jax.ShapeDtypeStruct(s, BF16) for s in shapes],
        in_specs=[VMEM] * len(operands),
        out_specs=[VMEM] * len(shapes),
        compiler_params=limit(8),
    )(*operands)


def join_kernel(mine_ref, mate_ref, out_ref):
    away = lax.axis_index("y") // 2 != lax.axis_index("core")
    other = mate_ref[...].reshape(mine_ref.shape)
    choose(away.astype(jnp.int32), (mine_ref[...], other), 0, out_ref)


def pack_kernel(far_ref, near_ref, out_ref):
    away = lax.axis_index("xh") != lax.axis_index("xl")
    half = near_ref.shape[0] // 2
    wide = [jnp.concatenate([r[...][:half], r[...][half:]], axis=1) for r in (near_ref, far_ref)]
    choose(away.astype(jnp.int32), wide, 0, out_ref)


def pair_kernel(up_ref, down_ref, out_ref, pick_ref):
    out_ref[...] = jnp.concatenate([up_ref[...], down_ref[...]], axis=0)
    for order, ref in enumerate((up_ref, down_ref)):

        @pl.when(lax.axis_index("core") == order)
        def _(ref=ref):
            pick_ref[...] = ref[...]


def stack(*parts):
    def kernel(*refs):
        refs[-1][...] = jnp.concatenate([r[...] for r in refs[:-1]], axis=0)

    return pl.pallas_call(
        kernel,
        out_shape=jax.ShapeDtypeStruct((sum(p.shape[0] for p in parts), parts[0].shape[1]), BF16),
        in_specs=[VMEM] * len(parts),
        out_specs=VMEM,
        compiler_params=limit(8),
    )(*parts)


def halves(*parts):
    depth = parts[0].shape[1] // 2

    def kernel(*refs):
        whole = jnp.concatenate([r[...] for r in refs[:-2]], axis=0)
        refs[-2][...] = whole[:, :depth]
        refs[-1][...] = whole[:, depth:]

    return local_call(kernel, [(sum(p.shape[0] for p in parts), depth)] * 2, *parts)


def low(*parts):
    def kernel(*refs):
        refs[-1][...] = jnp.concatenate([r[at:at + 20, :] for r, (_, at) in zip(refs, parts)], axis=0)

    rows = pl.pallas_call(
        kernel,
        out_shape=jax.ShapeDtypeStruct((20 * len(parts), parts[0][0].shape[1]), F32),
        in_specs=[VMEM] * len(parts),
        out_specs=VMEM,
        compiler_params=limit(8),
    )(*[p for p, _ in parts])
    return rows.astype(F16)


def last_kernel(in_ref, row_ref, col_ref, *refs):
    m0, m1, m2, m3, m4, b0, b2, b3, b4, out_ref, total, done, sems = refs
    here, z = lax.axis_index("y") % 2, lax.axis_index("z")
    there = 1 - here

    def put(shift, kept, at, back, start):
        total[lax.rem(z + shift + Z, Z)] = kept[at:at + 20, :] + back[start:start + 20, :]

    col = scale(col_ref[...])
    copies = []

    def leave(a):
        for n in range(2):
            rows = pl.ds(pl.multiple_of(a * 160 + n * 80, 80), 80)
            ladder = jnp.concatenate([total[i] for i in range(4 * n, 4 * n + 4)], axis=0)
            done[rows, :] = in_ref[rows, :] + (row_ref[rows, :1] * col) * ladder
            copies.append(pltpu.make_async_copy(done.at[rows], out_ref.at[rows], sems.at[len(copies)]))
            copies[-1].start()

    put(0, m0, 0, b0, 0)
    for step, h, at, b, start in ((1, m0, 80, b0, 40), (2, m1, 80, b2, 0), (3, m2, 80, b2, 80)):
        put(step, h, at, b, start)
        put(-step, h, at + 40, b, start + 20)
    put(4, m3, 80, b3, 40)
    leave(here)
    put(0, m0, 40, b0, 20)
    for step, s, b, start in ((1, m1, b0, 80), (2, m2, b2, 40), (3, m3, b3, 0)):
        put(step, s, 0, b, start)
        put(-step, s, 40, b, start + 20)
    put(4, m4, 0, b4, 0)
    leave(there)
    for copy in copies:
        copy.wait()


def finish(residual, row, col, parts):
    return pl.pallas_call(
        last_kernel,
        out_shape=jax.ShapeDtypeStruct(residual.shape, F32),
        in_specs=[VMEM] * (3 + len(parts)),
        out_specs=pl.BlockSpec(memory_space=pl.ANY),
        scratch_shapes=[
            pltpu.VMEM((Z, 20, residual.shape[1]), F32),
            pltpu.VMEM(residual.shape, F32),
            pltpu.SemaphoreType.DMA((4,)),
        ],
        compiler_params=limit(12),
    )(residual, row, col, *parts)


def fetch(x):
    def kernel(x_ref, out_ref, sem):
        copy = pltpu.make_async_copy(x_ref, out_ref, sem)
        copy.start()
        copy.wait()

    return pl.pallas_call(
        kernel,
        out_shape=jax.ShapeDtypeStruct(x.shape, x.dtype),
        in_specs=[pl.BlockSpec(memory_space=pl.ANY)],
        out_specs=VMEM,
        scratch_shapes=[pltpu.SemaphoreType.DMA],
        compiler_params=limit(1),
    )(x)


def scale(pairs):
    return jnp.where(pairs[0:1, :] == pairs[1:2, :], F32(0.5), F32(1.0))


def row_scale(pairs):
    count = pairs.shape[1]

    def kernel(pairs_ref, out_ref):
        out_ref[...] = jnp.broadcast_to(scale(pairs_ref[...]), (128, count)).T

    return pl.pallas_call(
        kernel,
        out_shape=jax.ShapeDtypeStruct((count, 128), F32),
        in_specs=[VMEM],
        out_specs=VMEM,
        compiler_params=limit(4),
    )(pairs)


def per_device(amplitudes, integrals, residual_in, pair_list, ab_list):
    tie = lax.optimization_barrier

    own = integrals.reshape(-1, integrals.shape[2])
    pairs, depth = amplitudes.shape[0], own.shape[0]
    block, double = (2 * pairs, 2 * depth), (4 * pairs, 2 * depth)

    mates, mine, own = tie((mate(amplitudes), amplitudes.reshape(pairs, depth), own))
    (both,) = local_call(join_kernel, [(2 * pairs, depth)], mine, mates)
    slots = spread(both, 1), spread(both, 0)
    other = mate(own)
    (held,) = local_call(pack_kernel, [block], *slots)

    def dot(*parts):
        left, right = halves(*parts)
        total = jnp.dot(left, own, preferred_element_type=F32)
        return total + jnp.dot(right, second, preferred_element_type=F32)

    above, below = up(held), down(held)
    swap0 = swap(held)
    above, below, second = tie((above, below, fetch(other)))
    old = above, below
    above, below = up(above), down(below)
    beside = stack(*old)
    swap1 = swap(beside)
    m0 = dot(held, swap0, beside)
    above, below, m0 = tie((above, below, m0))
    old = above, below
    above, below = up(above), down(below)
    beside = stack(*old)
    swap2 = swap(beside)
    m1 = dot(swap1, beside)
    goes0 = low((m0, 20), (m0, 60), (m0, 100), (m0, 140), (m1, 20), (m1, 60))
    above, below, m1, goes0 = tie((above, below, m1, goes0))
    beside, pick = local_call(pair_kernel, [double, block], above, below)
    opposite = either(pick)
    swap3 = swap(beside)
    b0 = trade(goes0)
    m2 = dot(swap2, beside)
    goes2 = low((m1, 100), (m1, 140), (m2, 20), (m2, 60), (m2, 100), (m2, 140))
    opposite, m2, goes2 = tie((opposite, m2, goes2))
    swap4 = swap(opposite)
    b2 = trade(goes2)
    m3 = dot(swap3, opposite)
    goes3 = low((m3, 20), (m3, 60), (m3, 100))
    swap4, m3, goes3 = tie((swap4, m3, goes3))
    b3 = trade(goes3)
    m4 = dot(swap4)
    goes4, pair_list, ab_list = tie((low((m4, 20)), pair_list.T, ab_list.T))
    b4 = trade(goes4)
    row = row_scale(pair_list)
    back = [b.astype(F32) for b in (b0, b2, b3, b4)]
    return finish(residual_in, row, ab_list, (m0, m1, m2, m3, m4, *back))


def solution(mesh):
    fine = Mesh(mesh.devices.reshape(XH, Y, Z, XL, 2), BLK + DS)
    placed = (P(BLK, None, DS), P(None, DS, BLK), P(DS, BLK), P(DS, None), P(BLK, None))
    return jax.shard_map(per_device, mesh=fine, in_specs=placed, out_specs=P(DS, BLK), check_vma=False)
```

```python
import jax
import jax.numpy as jnp
from jax import lax
from jax.experimental import pallas as pl
from jax.experimental.pallas import tpu as pltpu
from jax.sharding import Mesh
from jax.sharding import PartitionSpec as P

XH, Y, Z, XL = 2, 4, 8, 2
BLK = ("xh", "y", "z")
DS = ("xl", "core")
VMEM = pl.BlockSpec(memory_space=pltpu.VMEM)
F32, BF16, F16 = jnp.float32, jnp.bfloat16, jnp.float16
MIB = 1024 * 1024


def limit(size):
    return pltpu.CompilerParams(vmem_limit_bytes=size * MIB)


def turn(n, step):
    return [(i, (i + step) % n) for i in range(n)]


def up(x):
    return lax.ppermute(x, "z", turn(Z, -1))


def down(x):
    return lax.ppermute(x, "z", turn(Z, 1))


def either(x):
    route = [(2 * z + c, 2 * ((z + 2 * c - 1) % Z) + c) for z in range(Z) for c in range(2)]
    return lax.ppermute(x, ("z", "core"), route)


def swap(x):
    route = [(2 * y + c, 2 * (3 - y if c else y ^ 1) + c) for y in range(Y) for c in range(2)]
    return lax.ppermute(x, ("y", "core"), route)


def spread(x, flip):
    def at(x, y, c):
        return (x * Y + y) * 2 + c

    route = [(at(x, y, k), at(x ^ flip, y % 2 + 2 * k, y // 2)) for x in range(XH) for y in range(Y) for k in range(2)]
    return lax.ppermute(x, ("xh", "y", "core"), route)


def mate(x):
    return lax.ppermute(x, "core", turn(2, 1))


def trade(x):
    return lax.ppermute(x, "xl", turn(XL, 1))


def choose(first, pairs, axis, out_ref):
    for order, pair in enumerate((pairs, pairs[::-1])):

        @pl.when(first == order)
        def _(pair=pair):
            out_ref[...] = jnp.concatenate(pair, axis=axis)


def local_call(kernel, shapes, *operands):
    return pl.pallas_call(
        kernel,
        out_shape=[jax.ShapeDtypeStruct(s, BF16) for s in shapes],
        in_specs=[VMEM] * len(operands),
        out_specs=[VMEM] * len(shapes),
        compiler_params=limit(8),
    )(*operands)


def join_kernel(mine_ref, mate_ref, out_ref):
    away = lax.axis_index("y") // 2 != lax.axis_index("core")
    other = mate_ref[...].reshape(mine_ref.shape)
    choose(away.astype(jnp.int32), (mine_ref[...], other), 0, out_ref)


def pack_kernel(far_ref, near_ref, out_ref):
    away = lax.axis_index("xh") != lax.axis_index("xl")
    half = near_ref.shape[0] // 2
    wide = [jnp.concatenate([r[...][:half], r[...][half:]], axis=1) for r in (near_ref, far_ref)]
    choose(away.astype(jnp.int32), wide, 0, out_ref)


def pair_kernel(up_ref, down_ref, out_ref, pick_ref):
    out_ref[...] = jnp.concatenate([up_ref[...], down_ref[...]], axis=0)
    for order, ref in enumerate((up_ref, down_ref)):

        @pl.when(lax.axis_index("core") == order)
        def _(ref=ref):
            pick_ref[...] = ref[...]


def stack(*parts):
    def kernel(*refs):
        refs[-1][...] = jnp.concatenate([r[...] for r in refs[:-1]], axis=0)

    return pl.pallas_call(
        kernel,
        out_shape=jax.ShapeDtypeStruct((sum(p.shape[0] for p in parts), parts[0].shape[1]), BF16),
        in_specs=[VMEM] * len(parts),
        out_specs=VMEM,
        compiler_params=limit(8),
    )(*parts)


def halves(*parts):
    depth = parts[0].shape[1] // 2

    def kernel(*refs):
        whole = jnp.concatenate([r[...] for r in refs[:-2]], axis=0)
        refs[-2][...] = whole[:, :depth]
        refs[-1][...] = whole[:, depth:]

    return local_call(kernel, [(sum(p.shape[0] for p in parts), depth)] * 2, *parts)


def low(*parts):
    def kernel(*refs):
        refs[-1][...] = jnp.concatenate([r[at:at + 20, :] for r, (_, at) in zip(refs, parts)], axis=0)

    rows = pl.pallas_call(
        kernel,
        out_shape=jax.ShapeDtypeStruct((20 * len(parts), parts[0][0].shape[1]), F32),
        in_specs=[VMEM] * len(parts),
        out_specs=VMEM,
        compiler_params=limit(8),
    )(*[p for p, _ in parts])
    return rows.astype(F16)


def last_kernel(in_ref, row_ref, col_ref, *refs):
    m0, m1, m2, m3, m4, b0, b2, b3, b4, out_ref, total, done, sems = refs
    here, z = lax.axis_index("y") % 2, lax.axis_index("z")
    there = 1 - here

    def put(shift, kept, at, back, start):
        total[lax.rem(z + shift + Z, Z)] = kept[at:at + 20, :] + back[start:start + 20, :]

    col = scale(col_ref[...])
    copies = []

    def leave(a):
        for n in range(2):
            rows = pl.ds(pl.multiple_of(a * 160 + n * 80, 80), 80)
            ladder = jnp.concatenate([total[i] for i in range(4 * n, 4 * n + 4)], axis=0)
            done[rows, :] = in_ref[rows, :] + (row_ref[rows, :1] * col) * ladder
            copies.append(pltpu.make_async_copy(done.at[rows], out_ref.at[rows], sems.at[len(copies)]))
            copies[-1].start()

    put(0, m0, 0, b0, 0)
    for step, h, at, b, start in ((1, m0, 80, b0, 40), (2, m1, 80, b0, 120), (3, m2, 80, b2, 40)):
        put(step, h, at, b, start)
        put(-step, h, at + 40, b, start + 20)
    put(4, m3, 80, b3, 40)
    leave(here)
    put(0, m0, 40, b0, 20)
    for step, s, b, start in ((1, m1, b0, 80), (2, m2, b2, 0), (3, m3, b3, 0)):
        put(step, s, 0, b, start)
        put(-step, s, 40, b, start + 20)
    put(4, m4, 0, b4, 0)
    leave(there)
    for copy in copies:
        copy.wait()


def finish(residual, row, col, parts):
    return pl.pallas_call(
        last_kernel,
        out_shape=jax.ShapeDtypeStruct(residual.shape, F32),
        in_specs=[VMEM] * (3 + len(parts)),
        out_specs=pl.BlockSpec(memory_space=pl.ANY),
        scratch_shapes=[
            pltpu.VMEM((Z, 20, residual.shape[1]), F32),
            pltpu.VMEM(residual.shape, F32),
            pltpu.SemaphoreType.DMA((4,)),
        ],
        compiler_params=limit(12),
    )(residual, row, col, *parts)


def fetch(x):
    def kernel(x_ref, out_ref, sem):
        copy = pltpu.make_async_copy(x_ref, out_ref, sem)
        copy.start()
        copy.wait()

    return pl.pallas_call(
        kernel,
        out_shape=jax.ShapeDtypeStruct(x.shape, x.dtype),
        in_specs=[pl.BlockSpec(memory_space=pl.ANY)],
        out_specs=VMEM,
        scratch_shapes=[pltpu.SemaphoreType.DMA],
        compiler_params=limit(1),
    )(x)


def scale(pairs):
    return jnp.where(pairs[0:1, :] == pairs[1:2, :], F32(0.5), F32(1.0))


def row_scale(pairs):
    count = pairs.shape[1]

    def kernel(pairs_ref, out_ref):
        out_ref[...] = jnp.broadcast_to(scale(pairs_ref[...]), (128, count)).T

    return pl.pallas_call(
        kernel,
        out_shape=jax.ShapeDtypeStruct((count, 128), F32),
        in_specs=[VMEM],
        out_specs=VMEM,
        compiler_params=limit(4),
    )(pairs)


def per_device(amplitudes, integrals, residual_in, pair_list, ab_list):
    tie = lax.optimization_barrier

    own = integrals.reshape(-1, integrals.shape[2])
    pairs, depth = amplitudes.shape[0], own.shape[0]
    block, double = (2 * pairs, 2 * depth), (4 * pairs, 2 * depth)

    mates, mine, own = tie((mate(amplitudes), amplitudes.reshape(pairs, depth), own))
    (both,) = local_call(join_kernel, [(2 * pairs, depth)], mine, mates)
    slots = spread(both, 1), spread(both, 0)
    other = mate(own)
    (held,) = local_call(pack_kernel, [block], *slots)

    def dot(*parts):
        left, right = halves(*parts)
        total = jnp.dot(left, own, preferred_element_type=F32)
        return total + jnp.dot(right, second, preferred_element_type=F32)

    above, below = up(held), down(held)
    swap0 = swap(held)
    above, second = tie((above, fetch(other)))
    old = above, below
    above, below = up(above), down(below)
    beside = stack(*old)
    swap1 = swap(beside)
    m0 = dot(held, swap0, beside)
    below, m0 = tie((below, m0))
    old = above, below
    above, below = up(above), down(below)
    beside, swap1 = tie((stack(*old), swap1))
    swap2 = swap(beside)
    m1 = dot(swap1, beside)
    goes0 = low((m0, 20), (m0, 60), (m0, 100), (m0, 140), (m1, 20), (m1, 60), (m1, 100), (m1, 140))
    above, below, m1, goes0 = tie((above, below, m1, goes0))
    beside, pick = local_call(pair_kernel, [double, block], above, below)
    opposite = either(pick)
    swap3 = swap(beside)
    b0 = trade(goes0)
    m2 = dot(swap2, beside)
    goes2 = low((m2, 20), (m2, 60), (m2, 100), (m2, 140))
    opposite, m2, goes2 = tie((opposite, m2, goes2))
    swap4 = swap(opposite)
    b2 = trade(goes2)
    m3 = dot(swap3, opposite)
    goes3 = low((m3, 20), (m3, 60), (m3, 100))
    swap4, m3, goes3 = tie((swap4, m3, goes3))
    b3 = trade(goes3)
    m4 = dot(swap4)
    goes4, pair_list, ab_list = tie((low((m4, 20)), pair_list.T, ab_list.T))
    b4 = trade(goes4)
    row = row_scale(pair_list)
    back = [b.astype(F32) for b in (b0, b2, b3, b4)]
    return finish(residual_in, row, ab_list, (m0, m1, m2, m3, m4, *back))


def solution(mesh):
    fine = Mesh(mesh.devices.reshape(XH, Y, Z, XL, 2), BLK + DS)
    placed = (P(BLK, None, DS), P(None, DS, BLK), P(DS, BLK), P(DS, None), P(BLK, None))
    return jax.shard_map(per_device, mesh=fine, in_specs=placed, out_specs=P(DS, BLK), check_vma=False)
```

```python
import jax
import jax.numpy as jnp
from jax import lax
from jax.experimental import pallas as pl
from jax.experimental.pallas import tpu as pltpu
from jax.sharding import Mesh
from jax.sharding import PartitionSpec as P

XH, Y, Z, XL = 2, 4, 8, 2
BLK = ("xh", "y", "z")
DS = ("xl", "core")
VMEM = pl.BlockSpec(memory_space=pltpu.VMEM)
F32, BF16, F16 = jnp.float32, jnp.bfloat16, jnp.float16
MIB = 1024 * 1024


def limit(size):
    return pltpu.CompilerParams(vmem_limit_bytes=size * MIB)


def turn(n, step):
    return [(i, (i + step) % n) for i in range(n)]


def up(x):
    return lax.ppermute(x, "z", turn(Z, -1))


def down(x):
    return lax.ppermute(x, "z", turn(Z, 1))


def either(x):
    route = [(2 * z + c, 2 * ((z + 2 * c - 1) % Z) + c) for z in range(Z) for c in range(2)]
    return lax.ppermute(x, ("z", "core"), route)


def swap(x):
    route = [(2 * y + c, 2 * (3 - y if c else y ^ 1) + c) for y in range(Y) for c in range(2)]
    return lax.ppermute(x, ("y", "core"), route)


def spread(x, flip):
    def at(x, y, c):
        return (x * Y + y) * 2 + c

    route = [(at(x, y, k), at(x ^ flip, y % 2 + 2 * k, y // 2)) for x in range(XH) for y in range(Y) for k in range(2)]
    return lax.ppermute(x, ("xh", "y", "core"), route)


def mate(x):
    return lax.ppermute(x, "core", turn(2, 1))


def trade(x):
    return lax.ppermute(x, "xl", turn(XL, 1))


def choose(first, pairs, axis, out_ref):
    for order, pair in enumerate((pairs, pairs[::-1])):

        @pl.when(first == order)
        def _(pair=pair):
            out_ref[...] = jnp.concatenate(pair, axis=axis)


def local_call(kernel, shapes, *operands):
    return pl.pallas_call(
        kernel,
        out_shape=[jax.ShapeDtypeStruct(s, BF16) for s in shapes],
        in_specs=[VMEM] * len(operands),
        out_specs=[VMEM] * len(shapes),
        compiler_params=limit(8),
    )(*operands)


def join_kernel(mine_ref, mate_ref, out_ref):
    away = lax.axis_index("y") // 2 != lax.axis_index("core")
    other = mate_ref[...].reshape(mine_ref.shape)
    choose(away.astype(jnp.int32), (mine_ref[...], other), 0, out_ref)


def pack_kernel(far_ref, near_ref, out_ref):
    away = lax.axis_index("xh") != lax.axis_index("xl")
    half = near_ref.shape[0] // 2
    wide = [jnp.concatenate([r[...][:half], r[...][half:]], axis=1) for r in (near_ref, far_ref)]
    choose(away.astype(jnp.int32), wide, 0, out_ref)


def pair_kernel(up_ref, down_ref, out_ref, pick_ref):
    out_ref[...] = jnp.concatenate([up_ref[...], down_ref[...]], axis=0)
    for order, ref in enumerate((up_ref, down_ref)):

        @pl.when(lax.axis_index("core") == order)
        def _(ref=ref):
            pick_ref[...] = ref[...]


def stack(*parts):
    def kernel(*refs):
        refs[-1][...] = jnp.concatenate([r[...] for r in refs[:-1]], axis=0)

    return pl.pallas_call(
        kernel,
        out_shape=jax.ShapeDtypeStruct((sum(p.shape[0] for p in parts), parts[0].shape[1]), BF16),
        in_specs=[VMEM] * len(parts),
        out_specs=VMEM,
        compiler_params=limit(8),
    )(*parts)


def halves(*parts):
    depth = parts[0].shape[1] // 2

    def kernel(*refs):
        whole = jnp.concatenate([r[...] for r in refs[:-2]], axis=0)
        refs[-2][...] = whole[:, :depth]
        refs[-1][...] = whole[:, depth:]

    return local_call(kernel, [(sum(p.shape[0] for p in parts), depth)] * 2, *parts)


def low(*parts):
    def kernel(*refs):
        refs[-1][...] = jnp.concatenate([r[at:at + 20, :] for r, (_, at) in zip(refs, parts)], axis=0)

    rows = pl.pallas_call(
        kernel,
        out_shape=jax.ShapeDtypeStruct((20 * len(parts), parts[0][0].shape[1]), F32),
        in_specs=[VMEM] * len(parts),
        out_specs=VMEM,
        compiler_params=limit(8),
    )(*[p for p, _ in parts])
    return rows.astype(F16)


def last_kernel(in_ref, row_ref, col_ref, *refs):
    m0, m1, m2, m3, m4, b0, b3, b4, out_ref, total, done, sems = refs
    here, z = lax.axis_index("y") % 2, lax.axis_index("z")
    there = 1 - here

    def put(shift, kept, at, back, start):
        total[lax.rem(z + shift + Z, Z)] = kept[at:at + 20, :] + back[start:start + 20, :]

    col = scale(col_ref[...])
    copies = []

    def leave(a):
        for n in range(2):
            rows = pl.ds(pl.multiple_of(a * 160 + n * 80, 80), 80)
            ladder = jnp.concatenate([total[i] for i in range(4 * n, 4 * n + 4)], axis=0)
            done[rows, :] = in_ref[rows, :] + (row_ref[rows, :1] * col) * ladder
            copies.append(pltpu.make_async_copy(done.at[rows], out_ref.at[rows], sems.at[len(copies)]))
            copies[-1].start()

    put(0, m0, 0, b0, 0)
    for step, h, at, b, start in ((1, m0, 80, b0, 40), (2, m1, 80, b0, 120), (3, m2, 80, b3, 40)):
        put(step, h, at, b, start)
        put(-step, h, at + 40, b, start + 20)
    put(4, m3, 80, b3, 120)
    leave(here)
    put(0, m0, 40, b0, 20)
    for step, s, b, start in ((1, m1, b0, 80), (2, m2, b3, 0), (3, m3, b3, 80)):
        put(step, s, 0, b, start)
        put(-step, s, 40, b, start + 20)
    put(4, m4, 0, b4, 0)
    leave(there)
    for copy in copies:
        copy.wait()


def finish(residual, row, col, parts):
    return pl.pallas_call(
        last_kernel,
        out_shape=jax.ShapeDtypeStruct(residual.shape, F32),
        in_specs=[VMEM] * (3 + len(parts)),
        out_specs=pl.BlockSpec(memory_space=pl.ANY),
        scratch_shapes=[
            pltpu.VMEM((Z, 20, residual.shape[1]), F32),
            pltpu.VMEM(residual.shape, F32),
            pltpu.SemaphoreType.DMA((4,)),
        ],
        compiler_params=limit(12),
    )(residual, row, col, *parts)


def fetch(x):
    def kernel(x_ref, out_ref, sem):
        copy = pltpu.make_async_copy(x_ref, out_ref, sem)
        copy.start()
        copy.wait()

    return pl.pallas_call(
        kernel,
        out_shape=jax.ShapeDtypeStruct(x.shape, x.dtype),
        in_specs=[pl.BlockSpec(memory_space=pl.ANY)],
        out_specs=VMEM,
        scratch_shapes=[pltpu.SemaphoreType.DMA],
        compiler_params=limit(1),
    )(x)


def scale(pairs):
    return jnp.where(pairs[0:1, :] == pairs[1:2, :], F32(0.5), F32(1.0))


def row_scale(pairs):
    count = pairs.shape[1]

    def kernel(pairs_ref, out_ref):
        out_ref[...] = jnp.broadcast_to(scale(pairs_ref[...]), (128, count)).T

    return pl.pallas_call(
        kernel,
        out_shape=jax.ShapeDtypeStruct((count, 128), F32),
        in_specs=[VMEM],
        out_specs=VMEM,
        compiler_params=limit(4),
    )(pairs)


def per_device(amplitudes, integrals, residual_in, pair_list, ab_list):
    tie = lax.optimization_barrier

    own = integrals.reshape(-1, integrals.shape[2])
    pairs, depth = amplitudes.shape[0], own.shape[0]
    block, double = (2 * pairs, 2 * depth), (4 * pairs, 2 * depth)

    mates, mine, own = tie((mate(amplitudes), amplitudes.reshape(pairs, depth), own))
    (both,) = local_call(join_kernel, [(2 * pairs, depth)], mine, mates)
    slots = spread(both, 1), spread(both, 0)
    other = mate(own)
    (held,) = local_call(pack_kernel, [block], *slots)

    def dot(*parts):
        left, right = halves(*parts)
        total = jnp.dot(left, own, preferred_element_type=F32)
        return total + jnp.dot(right, second, preferred_element_type=F32)

    above, below = up(held), down(held)
    swap0 = swap(held)
    above, second = tie((above, fetch(other)))
    old = above, below
    above, below = up(above), down(below)
    beside = stack(*old)
    swap1 = swap(beside)
    m0 = dot(held, swap0, beside)
    below, m0 = tie((below, m0))
    old = above, below
    above, below = up(above), down(below)
    beside, swap1 = tie((stack(*old), swap1))
    swap2 = swap(beside)
    m1 = dot(swap1, beside)
    goes0 = low((m0, 20), (m0, 60), (m0, 100), (m0, 140), (m1, 20), (m1, 60), (m1, 100), (m1, 140))
    above, below, m1, goes0 = tie((above, below, m1, goes0))
    beside, pick = local_call(pair_kernel, [double, block], above, below)
    opposite = either(pick)
    swap3 = swap(beside)
    b0 = trade(goes0)
    m2 = dot(swap2, beside)
    opposite, m2 = tie((opposite, m2))
    swap4 = swap(opposite)
    m3 = dot(swap3, opposite)
    goes3 = low((m2, 20), (m2, 60), (m2, 100), (m2, 140), (m3, 20), (m3, 60), (m3, 100))
    swap4, m3, goes3 = tie((swap4, m3, goes3))
    b3 = trade(goes3)
    m4 = dot(swap4)
    goes4, pair_list, ab_list = tie((low((m4, 20)), pair_list.T, ab_list.T))
    b4 = trade(goes4)
    row = row_scale(pair_list)
    back = [b.astype(F32) for b in (b0, b3, b4)]
    return finish(residual_in, row, ab_list, (m0, m1, m2, m3, m4, *back))


def solution(mesh):
    fine = Mesh(mesh.devices.reshape(XH, Y, Z, XL, 2), BLK + DS)
    placed = (P(BLK, None, DS), P(None, DS, BLK), P(DS, BLK), P(DS, None), P(BLK, None))
    return jax.shard_map(per_device, mesh=fine, in_specs=placed, out_specs=P(DS, BLK), check_vma=False)
```
